32 devices in a mesh: grp: 4 (over z), shard: 8 (over y, x, core).
Axes of the slice: x: 2, y: 2, z: 4, core: 2. Of those that a mesh axis runs over, the one named last changes fastest.
Arguments:
- owner_shard: int32 [2, 4096, 16, 1], P(None, ('grp', 'shard')), may hold values from 0 to 7; in each aligned block of 2048 rows (0 to 2047, 2048 to 4095, ..., all dimensions but the last counted through in order) at most 512 rows name the same one
- local_row: int32 [2, 4096, 16], P(None, ('grp', 'shard')), may hold values from 0 to 511
- click_label: int32 [2, 4096], P(None, ('grp', 'shard')), may hold values 0 or 1
- row_table: float32 [4096, 128], P('shard'), may hold values from -3 to 3
- squared_sums: float32 [4096, 128], P('shard'), may hold values from 0.01 to 1
- w_input: bfloat16 [512, 1024], replicated, may hold values from -0.25 to 0.25
- w_hidden: bfloat16 [1024, 1024], replicated, may hold values from -0.1875 to 0.1875
- w_output: bfloat16 [1024], replicated, may hold values from -0.1875 to 0.1875
Outputs:
- new_table: float32 [4096, 128], P('shard')
- logits: float32 [2, 4096], P(None, ('grp', 'shard'))
- input_grad: float32 [524288], P(('grp', 'shard'))
The draws below stay inside these ranges and needn't reach their ends.
Inputs may be any that keep to these rules, and one draw needn't show every extreme that they name: `owner_shard`: within the ids of one device in one minibatch (aligned blocks of 2048 ids), at most 512 name the same owner shard, and that many do in some block.
All inputs are finite; a program needn't handle non-finite values. No bound on the sum of `click_label` on one device may be relied on, other than what follows from the above.
Results may differ from the reference program's by a relative error of at most 0.0039.
The reference program's roundings to bfloat16 on the way count: a program that leaves them out, or rounds other values in their place, can miss the bound.
Values may be sent and summed in bfloat16 or wider, within the bound.
A program may use at most 64 MiB of HBM per device.

```python
import math
import jax
import jax.numpy as jnp
import numpy as np
from jax import lax

E = 128
H = 1024
SLOTS = 4
HOT = 4
BATCHES = 2
TOK_DEV = 128
ROW_DEV = 512
LOOK = 16
CAP = 512
TOKENS = 4096
ROWS = 4096
N_SHARD = 8


def set_ends(array, own_key, low, top_value):
    extent = array.shape
    spot = [jax.random.randint(jax.random.fold_in(own_key, axis), (), 0, extent[axis]) for axis in range(len(extent))]
    array = array.at[tuple(spot)].set(low)
    longest = extent.index(max(extent))
    spot[longest] = (spot[longest] + 1) % extent[longest]
    return array.at[tuple(spot)].set(top_value)


def block_scale(stream_key, extent, cuts, smallest, largest):
    loudness = 1.0
    for position, shards_of in cuts:
        heights = jax.random.uniform(jax.random.fold_in(jax.random.fold_in(stream_key, 6), position), (shards_of,), jnp.float32, smallest / len(cuts), largest / len(cuts))
        loudness = loudness * jnp.repeat(jnp.exp(heights), extent[position] // shards_of).reshape((-1,) + (1,) * (len(extent) - 1 - position))
    return loudness


def rank_table(amount, skew):
    portions = [(1 << 20) // math.isqrt(rank ** skew) + 1 for rank in range(1, amount + 1)]
    spread = 1 + sum(portions) // (1 << 30)
    return np.cumsum(np.array([max(1, weight // spread) for weight in portions]))


def ranked_ids(rng, extent, number_of, skew):
    listing = rank_table(number_of, skew)
    ticket = jax.random.randint(jax.random.fold_in(rng, 1), extent, 0, int(listing[number_of - 1]))
    grade = jnp.searchsorted(jnp.asarray(listing, jnp.int32), ticket, side="right")
    return jax.random.permutation(jax.random.fold_in(rng, 2), number_of)[grade].astype(jnp.int32)


def assign_block(own_key, own, number, rows, number_of, top, most, lean):
    sequence = jax.random.permutation(own_key, number_of)
    packed, ordinary = portions_of(number_of, rows * top, most, lean, True), portions_of(number_of, rows * top, most, lean, False)
    places = jnp.arange(number_of)

    def named(sizes, offset_by):
        used = int((sizes > 0).sum())
        fixed = max(1, used // 4)
        shifted = fixed + (places - fixed + offset_by * (used - fixed)) % max(1, number_of - fixed)
        return jnp.zeros((number_of,), jnp.int32).at[sequence[jnp.where(places < fixed, places, shifted)]].set(jnp.asarray(sizes, jnp.int32))

    sizes = jnp.where(number % 4 == 0, named(packed, number // 4), named(ordinary, number - number // 4 - 1))
    mixed = jax.random.permutation(jax.random.fold_in(own, 3), number_of)
    source_of, receiver = mixed[0:number_of // 2 * 2:2], mixed[1:number_of // 2 * 2:2]
    slack = jnp.minimum(sizes[source_of] - 1, most - sizes[receiver]) // 2
    slack = jnp.where((source_of == sequence[0]) | (receiver == sequence[0]) | (sizes[receiver] == 0), 0, jnp.maximum(slack, 0))
    shifted = jax.random.randint(jax.random.fold_in(own, 4), (number_of // 2,), 0, 1 << 20) % (slack + 1)
    sizes = sizes.at[source_of].add(-shifted).at[receiver].add(shifted)
    members = jnp.searchsorted(jnp.cumsum(sizes), jnp.arange(rows * top), side="right").astype(jnp.int32)
    listing = members.reshape(top, rows).T
    listing = listing[jax.random.permutation(jax.random.fold_in(own, 1), rows)]
    offset_by = jax.random.randint(jax.random.fold_in(own, 2), (rows, 1), 0, top)
    return jnp.take_along_axis(listing, (jnp.arange(top)[None, :] + offset_by) % top, axis=1)


def portions_of(count, total, limit, lean, full):
    portions = [(1 << 20) // math.isqrt(rank ** lean) + 1 for rank in range(1, count + 1)]
    largest = limit if full else min(limit, max(-(-total // count), total * portions[0] // sum(portions)))
    least = 1 if total - largest >= count - 1 else 0
    given, rest = [largest] + [least] * (count - 1), total - largest - least * (count - 1)
    while rest > 0:
        movable = [i for i in range(1, count) if given[i] < largest] or [i for i in range(1, count) if given[i] < limit]
        pool, budget = sum([portions[i] for i in movable]), rest
        for i in movable:
            addition = min(limit - given[i], max(1, budget * portions[i] // pool), rest)
            given[i] = given[i] + addition
            rest = rest - addition
    return np.array(given)


def bell_draw(own_key, extent, spread, most, shards=(), held_as=jnp.bfloat16):
    result = jax.random.normal(own_key, extent, jnp.float32) * spread
    if len(shards) > 0:
        result = block_scale(own_key, extent, shards, -0.22, 0.18) * result
    return jnp.clip(result, min=-most, max=most).astype(held_as)


def setup_inputs(seed: int = 0) -> dict:
    key_list = jax.random.split(jax.random.key(seed), 9)
    owner_shard_keys = jax.random.split(jax.random.fold_in(key_list[0], 1), BATCHES * TOKENS * LOOK // (TOK_DEV * LOOK))
    owner_shard_turns = jax.random.permutation(jax.random.fold_in(key_list[0], 3), BATCHES * TOKENS * LOOK // (TOK_DEV * LOOK))
    owner_shard = jax.vmap(lambda own, number: assign_block(jax.random.fold_in(key_list[0], 2), own, number, TOK_DEV * LOOK, N_SHARD, 1, CAP, 2))(owner_shard_keys, owner_shard_turns).reshape((BATCHES, TOKENS, LOOK, 1))
    local_row = set_ends(ranked_ids(key_list[1], (BATCHES, TOKENS, LOOK), ROW_DEV, 2), jax.random.fold_in(key_list[1], 3), 0, ROW_DEV - 1).astype(jnp.int32)
    click_label = set_ends((jax.random.randint(key_list[2], (BATCHES, TOKENS), 0, 4) < 1).astype(jnp.int32), jax.random.fold_in(key_list[2], 1), 0, 1)
    row_table = bell_draw(key_list[3], (ROWS, E), 0.5, 3.0, ((0, 8),), jnp.float32)
    squared_sums = jnp.clip(jnp.exp(math.log(1.0) - 4.6051702 * jax.random.uniform(key_list[4], (ROWS, E), jnp.float32) ** block_scale(key_list[4], (ROWS, E), ((0, 8),), -0.2, 0.2)), 0.01, 1.0)
    w_input = bell_draw(key_list[5], (SLOTS * E, H), (SLOTS * E) ** -0.5, 0.25)
    w_hidden = bell_draw(key_list[6], (H, H), H ** -0.5, 0.1875)
    w_output = bell_draw(key_list[7], (H,), H ** -0.5, 0.1875)
    return dict(owner_shard=owner_shard, local_row=local_row, click_label=click_label, row_table=row_table, squared_sums=squared_sums, w_input=w_input, w_hidden=w_hidden, w_output=w_output)


learn_rate = 0.1

def mlp_pass(rows, labels, w_input, w_hidden, w_output):
    count = rows.shape[0]
    width = rows.shape[2]
    pooled = lax.optimization_barrier(jnp.sum(rows.reshape(count, SLOTS, HOT, width), axis=2, dtype=jnp.float32))
    pooled = pooled.astype(jnp.bfloat16).reshape(count, SLOTS * width)
    pre_one = jnp.dot(pooled, w_input, preferred_element_type=jnp.float32)
    act_one = jnp.maximum(pre_one, 0.0).astype(jnp.bfloat16)
    pre_two = jnp.dot(act_one, w_hidden, preferred_element_type=jnp.float32)
    act_two = jnp.maximum(pre_two, 0.0).astype(jnp.bfloat16)
    logits = jnp.dot(act_two, w_output, preferred_element_type=jnp.float32)
    slope = jax.nn.sigmoid(logits) - labels
    back_two = jnp.where(pre_two > 0, slope[:, None] * w_output.astype(jnp.float32)[None, :], 0.0).astype(jnp.bfloat16)
    back_one = lax.dot_general(back_two, w_hidden, (((1,), (1,)), ((), ())), preferred_element_type=jnp.float32)
    back_one = jnp.where(pre_one > 0, back_one, 0.0).astype(jnp.bfloat16)
    back_in = lax.dot_general(back_one, w_input, (((1,), (1,)), ((), ())), preferred_element_type=jnp.float32)
    back_in = back_in.astype(jnp.bfloat16)
    weight_term = lax.dot_general(pooled, back_one, (((0,), (0,)), ((), ())), preferred_element_type=jnp.float32)
    lookup_grad = jnp.broadcast_to(back_in.reshape(count, SLOTS, 1, width), (count, SLOTS, HOT, width))
    return (logits, lookup_grad.reshape(count * SLOTS * HOT, width), weight_term)

def reference(owner_shard, local_row, click_label, row_table, squared_sums, w_input, w_hidden, w_output):
    table_low = row_table.astype(jnp.bfloat16)
    global_id = (owner_shard[..., 0] * ROW_DEV + local_row).astype(jnp.int32)
    block = TOK_DEV * N_SHARD
    count = BATCHES * TOKENS // block
    id_blocks = global_id.reshape(count, block, LOOK)
    label_blocks = click_label.astype(jnp.float32).reshape(count, block)

    def one_block(carry, inputs):
        ids, labels = inputs
        grads, weights = carry
        logits, lookup_grad, weight_term = mlp_pass(table_low[ids], labels, w_input, w_hidden, w_output)
        grads = grads + jax.ops.segment_sum(lookup_grad.astype(jnp.float32), ids.reshape(-1), num_segments=ROWS)
        return ((grads, weights + weight_term), logits)
    start = (jnp.zeros((ROWS, E), jnp.float32), jnp.zeros((SLOTS * E, H), jnp.float32))
    (row_grad, input_grad), logits = lax.scan(one_block, start, (id_blocks, label_blocks))
    new_sums = squared_sums + row_grad * row_grad
    new_table = row_table - learn_rate * row_grad / jnp.sqrt(new_sums)
    return (new_table, logits.reshape(BATCHES, TOKENS), input_grad.reshape(-1))
```

```python
import jax
import jax.numpy as jnp
from jax import lax
from jax.sharding import PartitionSpec as P

SLOTS = 4
HOT = 4


learn_rate = 0.1


def mlp_pass(pooled, labels, w_input, w_hidden, w_output):
    pre_one = jnp.dot(pooled, w_input, preferred_element_type=jnp.float32)
    act_one = jnp.maximum(pre_one, 0.0).astype(jnp.bfloat16)
    pre_two = jnp.dot(act_one, w_hidden, preferred_element_type=jnp.float32)
    act_two = jnp.maximum(pre_two, 0.0).astype(jnp.bfloat16)
    logits = jnp.dot(act_two, w_output, preferred_element_type=jnp.float32)
    slope = jax.nn.sigmoid(logits) - labels
    back_two = jnp.where(
        pre_two > 0, slope[:, None] * w_output.astype(jnp.float32)[None, :], 0.0
    ).astype(jnp.bfloat16)
    back_one = lax.dot_general(
        back_two, w_hidden, (((1,), (1,)), ((), ())), preferred_element_type=jnp.float32
    )
    back_one = jnp.where(pre_one > 0, back_one, 0.0).astype(jnp.bfloat16)
    back_in = lax.dot_general(
        back_one, w_input, (((1,), (1,)), ((), ())), preferred_element_type=jnp.float32
    )
    back_in = back_in.astype(jnp.bfloat16)
    weight_term = lax.dot_general(
        pooled, back_one, (((0,), (0,)), ((), ())), preferred_element_type=jnp.float32
    )
    return (logits, back_in, weight_term)


def adagrad_step(table_part, sums_part, grad_part):
    new_sums = sums_part + grad_part * grad_part
    return table_part - learn_rate * grad_part / jnp.sqrt(new_sums)


def local(
    owner_shard, local_row, click_label, row_table, squared_sums, w_input, w_hidden, w_output
):
    row_count, width = row_table.shape
    batches, samples, looks = local_row.shape
    table_all = lax.all_gather(row_table.astype(jnp.bfloat16), "shard", axis=0, tiled=True)
    ids = (owner_shard[..., 0] * row_count + local_row).reshape(-1, HOT)
    rows = jnp.arange(table_all.shape[0], dtype=jnp.int32)
    counts = jnp.sum(
        (ids[:, :, None] == rows[None, None, :]).astype(jnp.float32), axis=1
    ).astype(jnp.bfloat16)
    pooled = jnp.dot(counts, table_all, preferred_element_type=jnp.float32)
    pooled = pooled.astype(jnp.bfloat16).reshape(batches * samples, SLOTS * width)
    labels = click_label.astype(jnp.float32).reshape(-1)
    logits, back_in, weight_term = mlp_pass(pooled, labels, w_input, w_hidden, w_output)
    row_part = lax.dot_general(
        counts,
        back_in.reshape(-1, width),
        (((0,), (0,)), ((), ())),
        preferred_element_type=jnp.float32,
    )
    row_grad = lax.psum_scatter(row_part, "shard", scatter_dimension=0, tiled=True)
    total = lax.psum(row_grad.astype(jnp.bfloat16), "grp").astype(jnp.float32)
    input_grad = lax.psum_scatter(
        weight_term.reshape(-1), ("grp", "shard"), scatter_dimension=0, tiled=True
    )
    new_table = adagrad_step(row_table, squared_sums, total)
    return (new_table, logits.reshape(batches, samples), input_grad)


def solution(mesh):
    in_specs = (
        P(None, ("grp", "shard"), None, None),
        P(None, ("grp", "shard"), None),
        P(None, ("grp", "shard")),
        P("shard", None),
        P("shard", None),
        P(),
        P(),
        P(),
    )
    out_specs = (P("shard", None), P(None, ("grp", "shard")), P(("grp", "shard")))
    return jax.shard_map(local, mesh=mesh, in_specs=in_specs, out_specs=out_specs, check_vma=False)
```

```python
import functools

import jax
import jax.numpy as jnp
from jax import lax
from jax.experimental import pallas as pl
from jax.experimental.pallas import tpu as pltpu
from jax.sharding import PartitionSpec as P

SLOTS = 4
HOT = 4
HALVES = 2
TILE = 256
MESH = pl.DeviceIdType.MESH

learn_rate = 0.1


def flip(index, mask):
    bit = 1
    while bit <= mask:
        if mask & bit:
            index = index + bit - 2 * bit * lax.rem(lax.div(index, bit), 2)
        bit *= 2
    return index


def bits_of(count):
    return [1 << i for i in range(count.bit_length() - 1)]


def high_first(order, place):
    relative = {"shard": 0, "grp": 0}
    for i, (axis, bit) in enumerate(order):
        if place >> (len(order) - 1 - i) & 1:
            relative[axis] |= bit
    return relative


def low_first(order, place):
    return high_first(order[::-1], place)


def kernel(
    n_shard,
    n_grp,
    keep,
    scatter,
    owner_ref,
    row_ref,
    label_ref,
    table_ref,
    sums_ref,
    w_in_hbm,
    w_hid_hbm,
    w_out_ref,
    new_ref,
    logit_ref,
    weight_ref,
    w_in,
    w_hid,
    gathered,
    keys,
    counts,
    lookups,
    pooled,
    pre_one,
    act_one,
    pre_two,
    act_two,
    back_two,
    back_one,
    row_sum,
    row_out,
    row_in,
    weight_term,
    weight_sum,
    weight_out,
    weight_in,
    load_sem,
    gather_send,
    gather_recv,
    row_send,
    row_recv,
    weight_send,
    weight_recv,
):
    samples = owner_ref.shape[0]
    rows, width = table_ref.shape
    hidden = w_hid.shape[0]
    half = rows // HALVES
    me = {"shard": lax.axis_index("shard"), "grp": lax.axis_index("grp")}
    shard_bits = [("shard", b) for b in bits_of(n_shard)]
    grp_bits = [("grp", b) for b in bits_of(n_grp)]
    near, far = shard_bits[:1], shard_bits[1:]
    gather_order = [far[::-1] + near, far + near]
    row_order = near + far
    weight_order = near + far[::-1] + grp_bits[::-1]

    def partner(step):
        axis, bit = step
        return {axis: flip(me[axis], bit)}

    load_in = pltpu.make_async_copy(w_in_hbm, w_in, load_sem.at[0])
    load_hid = pltpu.make_async_copy(w_hid_hbm, w_hid, load_sem.at[1])
    load_in.start()
    load_hid.start()

    barrier = pltpu.get_barrier_semaphore()
    for step in shard_bits + grp_bits:
        pl.semaphore_signal(barrier, inc=1, device_id=partner(step), device_id_type=MESH)
    for h in range(HALVES):
        gathered[h, 0] = table_ref[h * half : (h + 1) * half, :].astype(jnp.bfloat16)
    pl.semaphore_wait(barrier, len(shard_bits + grp_bits))

    started = []

    def send(source, target, send_sem, recv_sem, step):
        copy = pltpu.make_async_remote_copy(
            src_ref=source,
            dst_ref=target,
            send_sem=send_sem,
            recv_sem=recv_sem,
            device_id=partner(step),
            device_id_type=MESH,
        )
        copy.start()
        started.append(copy)
        return copy

    def gather_step(i):
        return [
            send(
                gathered.at[h, pl.ds(0, 1 << i)],
                gathered.at[h, pl.ds(1 << i, 1 << i)],
                gather_send.at[h, i],
                gather_recv.at[h, i],
                gather_order[h][i],
            )
            for h in range(HALVES)
        ]

    in_flight = gather_step(0)

    ids = owner_ref[...] * rows + row_ref[...]
    for j in range(SLOTS * HOT):
        keys[j] = jnp.broadcast_to(ids[:, j : j + 1], (samples, 128))

    lane = lax.broadcasted_iota(jnp.int32, (32, 128), 1)

    def build(h, place):
        relative = low_first(gather_order[h], place)["shard"]
        first = flip(me["shard"], relative) * rows + h * half
        block = counts.at[h * n_shard + place if keep else 0]

        def tile(t, _):
            at = pl.ds(pl.multiple_of(t * 32, 32), 32)
            for s in range(SLOTS):
                named = [keys[s * HOT + j, at, :] - first for j in range(HOT)]
                for c in range(half // 128):
                    hits = [jnp.where(k == lane + c * 128, 1.0, 0.0) for k in named]
                    total = (hits[0] + hits[1]) + (hits[2] + hits[3])
                    block[s, at, c * 128 : (c + 1) * 128] = total.astype(jnp.bfloat16)
            return 0

        lax.fori_loop(0, samples // 32, tile, 0)
        return block

    lookups[...] = jnp.zeros_like(lookups)

    def look_up(h, place, block):
        for s in range(SLOTS):
            lookups[s] += jnp.dot(
                block[s], gathered[h, place], preferred_element_type=jnp.float32
            )

    places = [(h, p) for p in range(n_shard) for h in range(HALVES)]
    steps = len(shard_bits)
    if keep:
        share = len(places) // steps
        for i in range(steps):
            end = len(places) if i == steps - 1 else (i + 1) * share
            for h, p in places[i * share : end]:
                build(h, p)
            for copy in in_flight:
                copy.wait_recv()
            if i < steps - 1:
                in_flight = gather_step(i + 1)
        for h, p in places:
            look_up(h, p, counts.at[h * n_shard + p])
    else:
        for i in range(steps):
            for copy in in_flight:
                copy.wait_recv()
            if i < steps - 1:
                in_flight = gather_step(i + 1)
        for h, p in places:
            look_up(h, p, build(h, p))

    for s in range(SLOTS):
        pooled[:, s * width : (s + 1) * width] = lookups[s].astype(jnp.bfloat16)
    columns = [slice(c, c + TILE) for c in range(0, hidden, TILE)]
    load_in.wait()
    for c in columns:
        value = jnp.dot(pooled[...], w_in[:, c], preferred_element_type=jnp.float32)
        pre_one[:, c] = value
        act_one[:, c] = jnp.maximum(value, 0.0).astype(jnp.bfloat16)
    load_hid.wait()
    out_row = w_out_ref[...].astype(jnp.float32)
    terms = jnp.zeros((samples, TILE), jnp.float32)
    for c in columns:
        value = jnp.dot(act_one[...], w_hid[:, c], preferred_element_type=jnp.float32)
        pre_two[:, c] = value
        acted = jnp.maximum(value, 0.0).astype(jnp.bfloat16).astype(jnp.float32)
        terms = terms + acted * out_row[:, c]
    logits = jnp.broadcast_to(jnp.sum(terms, axis=1, keepdims=True), (samples, 128))
    label = label_ref[...].astype(jnp.float32)
    batches, per_batch = label.shape
    label_columns = []
    for b in range(batches):
        at = slice(b * per_batch, (b + 1) * per_batch)
        logit_ref[b : b + 1, :] = jnp.transpose(logits[at, :])[0:1, :]
        label_columns.append(
            jnp.transpose(jnp.broadcast_to(label[b : b + 1, :], (128, per_batch)))
        )
    slope = (jax.nn.sigmoid(logits) - jnp.concatenate(label_columns, axis=0))[:, 0:1]
    for c in columns:
        back_two[:, c] = jnp.where(pre_two[:, c] > 0, slope * out_row[:, c], 0.0).astype(
            jnp.bfloat16
        )
    across = (((1,), (1,)), ((), ()))
    for c in columns:
        value = lax.dot_general(
            back_two[...], w_hid[c, :], across, preferred_element_type=jnp.float32
        )
        back_one[:, c] = jnp.where(pre_one[:, c] > 0, value, 0.0).astype(jnp.bfloat16)

    turned = jnp.transpose(pooled[...].astype(jnp.float32)).astype(jnp.bfloat16)
    total_ref = weight_term if scatter else weight_ref
    for c in columns:
        total_ref[:, c] = jnp.dot(turned, back_one[:, c], preferred_element_type=jnp.float32)

    weight_steps = len(weight_order) if scatter else 0
    chunks = 1 << weight_steps

    def weight_step(i):
        count = chunks >> (i + 1)
        at = pl.ds(chunks - 2 * count, count)
        return send(
            weight_out.at[at],
            weight_in.at[at],
            weight_send.at[i],
            weight_recv.at[i],
            weight_order[i],
        )

    def weight_add(i, copy):
        copy.wait_recv()
        count = chunks >> (i + 1)
        base = chunks - 2 * count
        weight_sum[0:count] += weight_in[base : base + count].astype(jnp.float32)
        if i < weight_steps - 1:
            left = count // 2
            weight_out[chunks - count : chunks - left] = weight_sum[left:count].astype(
                jnp.bfloat16
            )
            return weight_step(i + 1)
        return None

    weight_copy = None
    if scatter:
        depth = weight_sum.shape[1]

        def chunk_of(place):
            relative = high_first(weight_order, place)
            index = flip(me["grp"], relative["grp"]) * n_shard + flip(
                me["shard"], relative["shard"]
            )
            return weight_term[pl.ds(pl.multiple_of(index * depth, depth), depth), :]

        kept = chunks // 2
        for p in range(kept):
            weight_out[p] = chunk_of(kept + p).astype(jnp.bfloat16)
        weight_copy = weight_step(0)
        for p in range(kept):
            weight_sum[p] = chunk_of(p)

    back_in = [
        lax.dot_general(
            back_one[...],
            w_in[s * width : (s + 1) * width, :],
            across,
            preferred_element_type=jnp.float32,
        )
        .astype(jnp.bfloat16)
        .astype(jnp.float32)
        for s in range(SLOTS)
    ]
    back_turned = jnp.transpose(jnp.concatenate(back_in, axis=0)).astype(jnp.bfloat16)

    where_in = [
        {low_first(gather_order[h], p)["shard"]: p for p in range(n_shard)}
        for h in range(HALVES)
    ]

    def row_term(place, h):
        p = where_in[h][high_first(row_order, place)["shard"]]
        block = counts.at[h * n_shard + p] if keep else build(h, p)
        return jnp.dot(
            back_turned,
            block[...].reshape(SLOTS * samples, half),
            preferred_element_type=jnp.float32,
        )

    def row_step(i):
        count = n_shard >> (i + 1)
        at = pl.ds(n_shard - 2 * count, count)
        return send(row_out.at[at], row_in.at[at], row_send.at[i], row_recv.at[i], row_order[i])

    def row_add(i, copy):
        copy.wait_recv()
        count = n_shard >> (i + 1)
        base = n_shard - 2 * count
        row_sum[0:count] += row_in[base : base + count].astype(jnp.float32)
        left = count // 2
        if i < len(row_order) - 1:
            row_out[n_shard - count : n_shard - left] = row_sum[left:count].astype(jnp.bfloat16)
            return row_step(i + 1)
        return group_step(0)

    def group_step(i):
        place = n_shard - 1 + i
        row_out[place] = row_sum[0].astype(jnp.bfloat16)
        at = pl.ds(place, 1)
        k = len(row_order) + i
        return send(row_out.at[at], row_in.at[at], row_send.at[k], row_recv.at[k], grp_bits[i])

    def group_add(i, copy):
        copy.wait_recv()
        place = n_shard - 1 + i
        row_sum[0] = row_out[place].astype(jnp.float32) + row_in[place].astype(jnp.float32)
        return group_step(i + 1) if i < len(grp_bits) - 1 else None

    kept = n_shard // 2
    for p in range(kept):
        for h in range(HALVES):
            row_out[p, :, h * half : (h + 1) * half] = row_term(kept + p, h).astype(jnp.bfloat16)
    row_copy = row_step(0)
    for p in range(kept):
        for h in range(HALVES):
            row_sum[p, :, h * half : (h + 1) * half] = row_term(p, h)

    adds = [functools.partial(row_add, i) for i in range(len(row_order))]
    adds += [functools.partial(group_add, i) for i in range(len(grp_bits))]
    for i in range(max(len(adds), weight_steps)):
        if i < weight_steps:
            weight_copy = weight_add(i, weight_copy)
        if i < len(adds):
            row_copy = adds[i](row_copy)

    if scatter:
        lines = hidden // 128
        for j in range(lines):
            weight_ref[pl.ds(j, depth, stride=lines), :] = weight_sum[
                0, :, j * 128 : (j + 1) * 128
            ]
    grad = jnp.transpose(row_sum[0])
    new_sums = sums_ref[...] + grad * grad
    new_ref[...] = table_ref[...] - learn_rate * grad / jnp.sqrt(new_sums)
    for copy in started:
        copy.wait_send()


def local(
    n_shard,
    n_grp,
    owner_shard,
    local_row,
    click_label,
    row_table,
    squared_sums,
    w_input,
    w_hidden,
    w_output,
):
    rows, width = row_table.shape
    batches, per_batch, looks = local_row.shape
    samples = batches * per_batch
    wide, hidden = w_input.shape
    depth = wide // (n_shard * n_grp)
    scatter = depth > 0 and depth % 16 == 0
    keep = n_shard <= 8
    half = rows // HALVES
    chunks = n_shard * n_grp if scatter else 1
    depth = depth if scatter else 16
    shard_steps = n_shard.bit_length() - 1
    grp_steps = n_grp.bit_length() - 1
    row_slots = n_shard - 1 + grp_steps
    vmem = pl.BlockSpec(memory_space=pltpu.VMEM)
    hbm = pl.BlockSpec(memory_space=pl.ANY)
    low = jnp.bfloat16
    full = jnp.float32
    weight_shape = (depth * hidden // 128, 128) if scatter else (wide, hidden)
    new_table, logits, weight = pl.pallas_call(
        functools.partial(kernel, n_shard, n_grp, keep, scatter),
        out_shape=(
            jax.ShapeDtypeStruct((rows, width), full),
            jax.ShapeDtypeStruct((batches, per_batch), full),
            jax.ShapeDtypeStruct(weight_shape, full),
        ),
        in_specs=[vmem, vmem, vmem, vmem, vmem, hbm, hbm, vmem],
        out_specs=(vmem, vmem, vmem),
        scratch_shapes=[
            pltpu.VMEM((wide, hidden), low),
            pltpu.VMEM((hidden, hidden), low),
            pltpu.VMEM((HALVES, n_shard, half, width), low),
            pltpu.VMEM((looks, samples, 128), jnp.int32),
            pltpu.VMEM((HALVES * n_shard if keep else 1, SLOTS, samples, half), low),
            pltpu.VMEM((SLOTS, samples, width), full),
            pltpu.VMEM((samples, wide), low),
            pltpu.VMEM((samples, hidden), full),
            pltpu.VMEM((samples, hidden), low),
            pltpu.VMEM((samples, hidden), full),
            pltpu.VMEM((16, 128), low),
            pltpu.VMEM((samples, hidden), low),
            pltpu.VMEM((samples, hidden), low),
            pltpu.VMEM((n_shard // 2, width, rows), full),
            pltpu.VMEM((row_slots, width, rows), low),
            pltpu.VMEM((row_slots, width, rows), low),
            pltpu.VMEM((wide, hidden) if scatter else (8, 128), full),
            pltpu.VMEM((max(1, chunks // 2), depth, hidden), full),
            pltpu.VMEM((max(1, chunks - 1), depth, hidden), low),
            pltpu.VMEM((max(1, chunks - 1), depth, hidden), low),
            pltpu.SemaphoreType.DMA((2,)),
            pltpu.SemaphoreType.DMA((HALVES, shard_steps)),
            pltpu.SemaphoreType.DMA((HALVES, shard_steps)),
            pltpu.SemaphoreType.DMA((shard_steps + grp_steps,)),
            pltpu.SemaphoreType.DMA((shard_steps + grp_steps,)),
            pltpu.SemaphoreType.DMA((shard_steps + grp_steps,)),
            pltpu.SemaphoreType.DMA((shard_steps + grp_steps,)),
        ],
        compiler_params=pltpu.CompilerParams(
            collective_id=0, has_side_effects=True, vmem_limit_bytes=56 * 1024 * 1024
        ),
    )(
        owner_shard.reshape(samples, looks),
        local_row.reshape(samples, looks),
        click_label,
        row_table,
        squared_sums,
        w_input,
        w_hidden,
        w_output.reshape(1, hidden),
    )
    weight = weight.reshape(-1)
    if not scatter:
        weight = lax.psum_scatter(weight, ("grp", "shard"), scatter_dimension=0, tiled=True)
    return (new_table, logits, weight)


def solution(mesh):
    in_specs = (
        P(None, ("grp", "shard"), None, None),
        P(None, ("grp", "shard"), None),
        P(None, ("grp", "shard")),
        P("shard", None),
        P("shard", None),
        P(),
        P(),
        P(),
    )
    out_specs = (P("shard", None), P(None, ("grp", "shard")), P(("grp", "shard")))
    part = functools.partial(local, mesh.shape["shard"], mesh.shape["grp"])
    return jax.shard_map(part, mesh=mesh, in_specs=in_specs, out_specs=out_specs, check_vma=False)
```

```python
import functools

import jax
import jax.numpy as jnp
from jax import lax
from jax.experimental import pallas as pl
from jax.experimental.pallas import tpu as pltpu
from jax.sharding import PartitionSpec as P

SLOTS = 4
HOT = 4
HALVES = 2
TILE = 256
MESH = pl.DeviceIdType.MESH

learn_rate = 0.1


def flip(index, mask):
    bit = 1
    while bit <= mask:
        if mask & bit:
            index = index + bit - 2 * bit * lax.rem(lax.div(index, bit), 2)
        bit *= 2
    return index


def bits_of(count):
    return [1 << i for i in range(count.bit_length() - 1)]


def high_first(order, place):
    relative = {"shard": 0, "grp": 0}
    for i, (axis, bit) in enumerate(order):
        if place >> (len(order) - 1 - i) & 1:
            relative[axis] |= bit
    return relative


def low_first(order, place):
    return high_first(order[::-1], place)


def kernel(
    n_shard,
    n_grp,
    keep,
    scatter,
    owner_ref,
    row_ref,
    label_ref,
    table_ref,
    sums_ref,
    w_in_hbm,
    w_hid_hbm,
    w_out_ref,
    new_ref,
    logit_ref,
    weight_ref,
    w_in,
    w_hid,
    gathered,
    keys,
    counts,
    lookups,
    pooled,
    pre_one,
    act_one,
    pre_two,
    back_two,
    back_one,
    row_sum,
    row_out,
    row_in,
    grad,
    part_out,
    part_in,
    part_all,
    weight_term,
    weight_sum,
    weight_out,
    weight_in,
    load_sem,
    gather_send,
    gather_recv,
    row_send,
    row_recv,
    part_send,
    part_recv,
    weight_send,
    weight_recv,
):
    looks = SLOTS * HOT
    batches, per_batch = label_ref.shape
    samples = batches * per_batch
    rows, width = table_ref.shape
    hidden = w_hid.shape[0]
    half = rows // HALVES
    me = {"shard": lax.axis_index("shard"), "grp": lax.axis_index("grp")}
    shard_bits = [("shard", b) for b in bits_of(n_shard)]
    grp_bits = [("grp", b) for b in bits_of(n_grp)]
    near, far = shard_bits[:1], shard_bits[1:]
    gather_order = [far[::-1] + near, far + near]
    row_order = near + far
    weight_order = near + far[::-1] + grp_bits

    def partner(step):
        axis, bit = step
        return {axis: flip(me[axis], bit)}

    load_in = pltpu.make_async_copy(w_in_hbm, w_in, load_sem.at[0])
    load_hid = pltpu.make_async_copy(w_hid_hbm, w_hid, load_sem.at[1])
    load_in.start()
    load_hid.start()

    barrier = pltpu.get_barrier_semaphore()
    peers = [("grp", relative) for relative in range(1, n_grp)]
    for step in shard_bits + peers:
        pl.semaphore_signal(barrier, inc=1, device_id=partner(step), device_id_type=MESH)
    for h in range(HALVES):
        gathered[h, 0] = table_ref[h * half : (h + 1) * half, :].astype(jnp.bfloat16)
    pl.semaphore_wait(barrier, len(shard_bits + peers))

    started = []

    def send(source, target, send_sem, recv_sem, step):
        copy = pltpu.make_async_remote_copy(
            src_ref=source,
            dst_ref=target,
            send_sem=send_sem,
            recv_sem=recv_sem,
            device_id=partner(step),
            device_id_type=MESH,
        )
        copy.start()
        started.append(copy)
        return copy

    def gather_step(i):
        return [
            send(
                gathered.at[h, pl.ds(0, 1 << i)],
                gathered.at[h, pl.ds(1 << i, 1 << i)],
                gather_send.at[h, i],
                gather_recv.at[h, i],
                gather_order[h][i],
            )
            for h in range(HALVES)
        ]

    in_flight = gather_step(0)

    ids = owner_ref[...] * rows + row_ref[...]
    for b in range(batches):
        turned_ids = jnp.transpose(ids[b * looks : (b + 1) * looks, :])
        for j in range(looks):
            keys[j, b * per_batch : (b + 1) * per_batch, :] = jnp.broadcast_to(
                turned_ids[:, j : j + 1], (per_batch, 128)
            ).astype(jnp.int16)

    lane = lax.broadcasted_iota(jnp.int32, (32, 128), 1)
    one = jnp.ones((32, 128), jnp.bfloat16)
    none = jnp.zeros((32, 128), jnp.bfloat16)

    def build(h, place):
        relative = low_first(gather_order[h], place)["shard"]
        first = flip(me["shard"], relative) * rows + h * half
        block = counts.at[h * n_shard + place if keep else 0]
        lanes = [(lane + (first + c * 128)).astype(jnp.int16) for c in range(half // 128)]

        def tile(t, _):
            at = pl.ds(pl.multiple_of(t * 32, 32), 32)
            for s in range(SLOTS):
                named = [keys[s * HOT + j, at, :] for j in range(HOT)]
                for c in range(half // 128):
                    hits = [jnp.where(k == lanes[c], one, none) for k in named]
                    total = (hits[0] + hits[1]) + (hits[2] + hits[3])
                    block[s, at, c * 128 : (c + 1) * 128] = total
            return 0

        lax.fori_loop(0, samples // 32, tile, 0)
        return block

    lookups[...] = jnp.zeros_like(lookups)

    def look_up(h, place, block):
        for s in range(SLOTS):
            lookups[s] += jnp.dot(
                block[s], gathered[h, place], preferred_element_type=jnp.float32
            )

    places = [(h, p) for p in range(n_shard) for h in range(HALVES)]
    steps = len(shard_bits)
    if keep:
        share = len(places) // steps
        for i in range(steps):
            end = len(places) if i == steps - 1 else (i + 1) * share
            for h, p in places[i * share : end]:
                build(h, p)
            for copy in in_flight:
                copy.wait_recv()
            if i < steps - 1:
                in_flight = gather_step(i + 1)
        for h, p in places:
            look_up(h, p, counts.at[h * n_shard + p])
    else:
        for i in range(steps):
            for copy in in_flight:
                copy.wait_recv()
            if i < steps - 1:
                in_flight = gather_step(i + 1)
        for h, p in places:
            look_up(h, p, build(h, p))

    for s in range(SLOTS):
        pooled[:, s * width : (s + 1) * width] = lookups[s].astype(jnp.bfloat16)
    columns = [slice(c, c + TILE) for c in range(0, hidden, TILE)]
    load_in.wait()
    for c in columns:
        value = jnp.dot(pooled[...], w_in[:, c], preferred_element_type=jnp.float32)
        pre_one[:, c] = value
        act_one[:, c] = jnp.maximum(value, 0.0).astype(jnp.bfloat16)
    load_hid.wait()
    out_lines = w_out_ref[...].astype(jnp.float32)
    out_row = jnp.concatenate([out_lines[i : i + 1, :] for i in range(hidden // 128)], axis=1)
    terms = jnp.zeros((samples, TILE), jnp.float32)
    for c in columns:
        value = jnp.dot(act_one[...], w_hid[:, c], preferred_element_type=jnp.float32)
        pre_two[:, c] = value
        acted = jnp.maximum(value, 0.0).astype(jnp.bfloat16).astype(jnp.float32)
        terms = terms + acted * out_row[:, c]
    logits = jnp.broadcast_to(jnp.sum(terms, axis=1, keepdims=True), (samples, 128))
    label = label_ref[...].astype(jnp.float32)
    label_columns = []
    for b in range(batches):
        at = slice(b * per_batch, (b + 1) * per_batch)
        logit_ref[b : b + 1, :] = jnp.transpose(logits[at, :])[0:1, :]
        label_columns.append(
            jnp.transpose(jnp.broadcast_to(label[b : b + 1, :], (128, per_batch)))
        )
    slope = (jax.nn.sigmoid(logits) - jnp.concatenate(label_columns, axis=0))[:, 0:1]
    for c in columns:
        back_two[:, c] = jnp.where(pre_two[:, c] > 0, slope * out_row[:, c], 0.0).astype(
            jnp.bfloat16
        )
    across = (((1,), (1,)), ((), ()))
    for c in columns:
        value = lax.dot_general(
            back_two[...], w_hid[c, :], across, preferred_element_type=jnp.float32
        )
        back_one[:, c] = jnp.where(pre_one[:, c] > 0, value, 0.0).astype(jnp.bfloat16)

    turned = jnp.transpose(pooled[...].astype(jnp.float32)).astype(jnp.bfloat16)
    total_ref = weight_term if scatter else weight_ref
    for c in columns:
        total_ref[:, c] = jnp.dot(turned, back_one[:, c], preferred_element_type=jnp.float32)

    weight_steps = len(weight_order) if scatter else 0
    chunks = 1 << weight_steps

    def weight_step(i):
        count = chunks >> (i + 1)
        at = pl.ds(chunks - 2 * count, count)
        return send(
            weight_out.at[at],
            weight_in.at[at],
            weight_send.at[i],
            weight_recv.at[i],
            weight_order[i],
        )

    def weight_add(i, copy):
        copy.wait_recv()
        count = chunks >> (i + 1)
        base = chunks - 2 * count
        weight_sum[0:count] += weight_in[base : base + count].astype(jnp.float32)
        if i < weight_steps - 1:
            left = count // 2
            weight_out[chunks - count : chunks - left] = weight_sum[left:count].astype(
                jnp.bfloat16
            )
            return weight_step(i + 1)
        return None

    weight_copy = None
    if scatter:
        depth = weight_sum.shape[1]

        def chunk_of(place):
            relative = high_first(weight_order, place)
            index = flip(me["grp"], relative["grp"]) * n_shard + flip(
                me["shard"], relative["shard"]
            )
            return weight_term[pl.ds(pl.multiple_of(index * depth, depth), depth), :]

        kept = chunks // 2
        for p in range(kept):
            weight_out[p] = chunk_of(kept + p).astype(jnp.bfloat16)
        weight_copy = weight_step(0)
        for p in range(kept):
            weight_sum[p] = chunk_of(p)

    back_in = [
        lax.dot_general(
            back_one[...],
            w_in[s * width : (s + 1) * width, :],
            across,
            preferred_element_type=jnp.float32,
        )
        .astype(jnp.bfloat16)
        .astype(jnp.float32)
        for s in range(SLOTS)
    ]
    back_turned = jnp.transpose(jnp.concatenate(back_in, axis=0)).astype(jnp.bfloat16)

    where_in = [
        {low_first(gather_order[h], p)["shard"]: p for p in range(n_shard)}
        for h in range(HALVES)
    ]

    def row_term(place, h):
        p = where_in[h][high_first(row_order, place)["shard"]]
        block = counts.at[h * n_shard + p] if keep else build(h, p)
        return jnp.dot(
            back_turned,
            block[...].reshape(SLOTS * samples, half),
            preferred_element_type=jnp.float32,
        )

    def row_step(i):
        count = n_shard >> (i + 1)
        at = pl.ds(n_shard - 2 * count, count)
        return send(row_out.at[at], row_in.at[at], row_send.at[i], row_recv.at[i], row_order[i])

    def row_add(i, copy):
        copy.wait_recv()
        count = n_shard >> (i + 1)
        base = n_shard - 2 * count
        row_sum[0:count] += row_in[base : base + count].astype(jnp.float32)
        left = count // 2
        if i < len(row_order) - 1:
            row_out[n_shard - count : n_shard - left] = row_sum[left:count].astype(jnp.bfloat16)
            return row_step(i + 1)
        return group_send()

    part = rows // n_grp

    def rows_of(relative):
        at = flip(me["grp"], relative) * part
        return pl.ds(pl.multiple_of(at, part), part)

    def group_send():
        grad[...] = jnp.transpose(row_sum[0])
        copies = []
        for i, step in enumerate(peers):
            part_out[i] = grad[rows_of(step[1]), :].astype(jnp.bfloat16)
            copies.append(
                send(
                    part_out.at[i],
                    part_in.at[i],
                    part_send.at[0, i],
                    part_recv.at[0, i],
                    step,
                )
            )
        return copies

    def group_sum(copies):
        total = grad[rows_of(0), :]
        for i, copy in enumerate(copies):
            copy.wait_recv()
            total = total + part_in[i].astype(jnp.float32)
        part_all[0] = total.astype(jnp.bfloat16)
        return [
            send(
                part_all.at[0],
                part_all.at[step[1]],
                part_send.at[1, i],
                part_recv.at[1, i],
                step,
            )
            for i, step in enumerate(peers)
        ]

    kept = n_shard // 2
    for p in range(kept):
        for h in range(HALVES):
            row_out[p, :, h * half : (h + 1) * half] = row_term(kept + p, h).astype(jnp.bfloat16)
    row_copy = row_step(0)
    for p in range(kept):
        for h in range(HALVES):
            row_sum[p, :, h * half : (h + 1) * half] = row_term(p, h)

    for i in range(len(row_order)):
        if scatter:
            weight_copy = weight_add(i, weight_copy)
        row_copy = row_add(i, row_copy)
    weight_left = list(range(len(row_order), weight_steps))
    for i in weight_left[:1]:
        weight_copy = weight_add(i, weight_copy)
    row_copy = group_sum(row_copy)
    for i in weight_left[1:]:
        weight_copy = weight_add(i, weight_copy)

    if scatter:
        lines = hidden // 128
        for j in range(lines):
            weight_ref[pl.ds(j, depth, stride=lines), :] = weight_sum[
                0, :, j * 128 : (j + 1) * 128
            ]
    for i in range(n_grp):
        if i > 0:
            row_copy[i - 1].wait_recv()
        at = rows_of(i)
        term = part_all[i].astype(jnp.float32)
        new_sums = sums_ref[at, :] + term * term
        new_ref[at, :] = table_ref[at, :] - learn_rate * term / jnp.sqrt(new_sums)
    for copy in started:
        copy.wait_send()


def local(
    n_shard,
    n_grp,
    owner_shard,
    local_row,
    click_label,
    row_table,
    squared_sums,
    w_input,
    w_hidden,
    w_output,
):
    rows, width = row_table.shape
    batches, per_batch, looks = local_row.shape
    samples = batches * per_batch
    wide, hidden = w_input.shape
    depth = wide // (n_shard * n_grp)
    scatter = depth > 0 and depth % 16 == 0
    keep = n_shard <= 8
    half = rows // HALVES
    chunks = n_shard * n_grp if scatter else 1
    depth = depth if scatter else 16
    shard_steps = n_shard.bit_length() - 1
    grp_steps = n_grp.bit_length() - 1
    part = rows // n_grp
    vmem = pl.BlockSpec(memory_space=pltpu.VMEM)
    hbm = pl.BlockSpec(memory_space=pl.ANY)
    low = jnp.bfloat16
    full = jnp.float32
    weight_shape = (depth * hidden // 128, 128) if scatter else (wide, hidden)
    new_table, logits, weight = pl.pallas_call(
        functools.partial(kernel, n_shard, n_grp, keep, scatter),
        out_shape=(
            jax.ShapeDtypeStruct((rows, width), full),
            jax.ShapeDtypeStruct((batches, per_batch), full),
            jax.ShapeDtypeStruct(weight_shape, full),
        ),
        in_specs=[vmem, vmem, vmem, vmem, vmem, hbm, hbm, vmem],
        out_specs=(vmem, vmem, vmem),
        scratch_shapes=[
            pltpu.VMEM((wide, hidden), low),
            pltpu.VMEM((hidden, hidden), low),
            pltpu.VMEM((HALVES, n_shard, half, width), low),
            pltpu.VMEM((looks, samples, 128), jnp.int16),
            pltpu.VMEM((HALVES * n_shard if keep else 1, SLOTS, samples, half), low),
            pltpu.VMEM((SLOTS, samples, width), full),
            pltpu.VMEM((samples, wide), low),
            pltpu.VMEM((samples, hidden), full),
            pltpu.VMEM((samples, hidden), low),
            pltpu.VMEM((samples, hidden), full),
            pltpu.VMEM((samples, hidden), low),
            pltpu.VMEM((samples, hidden), low),
            pltpu.VMEM((n_shard // 2, width, rows), full),
            pltpu.VMEM((n_shard - 1, width, rows), low),
            pltpu.VMEM((n_shard - 1, width, rows), low),
            pltpu.VMEM((rows, width), full),
            pltpu.VMEM((n_grp - 1, part, width), low),
            pltpu.VMEM((n_grp - 1, part, width), low),
            pltpu.VMEM((n_grp, part, width), low),
            pltpu.VMEM((wide, hidden) if scatter else (8, 128), full),
            pltpu.VMEM((max(1, chunks // 2), depth, hidden), full),
            pltpu.VMEM((max(1, chunks - 1), depth, hidden), low),
            pltpu.VMEM((max(1, chunks - 1), depth, hidden), low),
            pltpu.SemaphoreType.DMA((2,)),
            pltpu.SemaphoreType.DMA((HALVES, shard_steps)),
            pltpu.SemaphoreType.DMA((HALVES, shard_steps)),
            pltpu.SemaphoreType.DMA((shard_steps,)),
            pltpu.SemaphoreType.DMA((shard_steps,)),
            pltpu.SemaphoreType.DMA((2, n_grp - 1)),
            pltpu.SemaphoreType.DMA((2, n_grp - 1)),
            pltpu.SemaphoreType.DMA((shard_steps + grp_steps,)),
            pltpu.SemaphoreType.DMA((shard_steps + grp_steps,)),
        ],
        compiler_params=pltpu.CompilerParams(
            collective_id=0, has_side_effects=True, vmem_limit_bytes=56 * 1024 * 1024
        ),
    )(
        jnp.transpose(owner_shard, (0, 2, 3, 1)).reshape(batches * looks, per_batch),
        jnp.transpose(local_row, (0, 2, 1)).reshape(batches * looks, per_batch),
        click_label,
        row_table,
        squared_sums,
        w_input,
        w_hidden,
        w_output.reshape(hidden // 128, 128),
    )
    weight = weight.reshape(-1)
    if not scatter:
        weight = lax.psum_scatter(weight, ("grp", "shard"), scatter_dimension=0, tiled=True)
    return (new_table, logits, weight)


def solution(mesh):
    in_specs = (
        P(None, ("grp", "shard"), None, None),
        P(None, ("grp", "shard"), None),
        P(None, ("grp", "shard")),
        P("shard", None),
        P("shard", None),
        P(),
        P(),
        P(),
    )
    out_specs = (P("shard", None), P(None, ("grp", "shard")), P(("grp", "shard")))
    part = functools.partial(local, mesh.shape["shard"], mesh.shape["grp"])
    return jax.shard_map(part, mesh=mesh, in_specs=in_specs, out_specs=out_specs, check_vma=False)
```

```python
import functools

import jax
import jax.numpy as jnp
from jax import lax
from jax.experimental import pallas as pl
from jax.experimental.pallas import tpu as pltpu
from jax.sharding import PartitionSpec as P

SLOTS = 4
HOT = 4
HALVES = 2
TILE = 256
MESH = pl.DeviceIdType.MESH

learn_rate = 0.1


def flip(index, mask):
    bit = 1
    while bit <= mask:
        if mask & bit:
            index = index + bit - 2 * bit * lax.rem(lax.div(index, bit), 2)
        bit *= 2
    return index


def bits_of(count):
    return [1 << i for i in range(count.bit_length() - 1)]


def high_first(order, place):
    relative = {"shard": 0, "grp": 0}
    for i, (axis, bit) in enumerate(order):
        if place >> (len(order) - 1 - i) & 1:
            relative[axis] |= bit
    return relative


def low_first(order, place):
    return high_first(order[::-1], place)


def kernel(
    n_shard,
    n_grp,
    keep,
    scatter,
    owner_ref,
    row_ref,
    label_ref,
    table_ref,
    sums_ref,
    w_in_hbm,
    w_hid_hbm,
    w_out_ref,
    new_ref,
    logit_ref,
    weight_ref,
    w_in,
    w_hid,
    gathered,
    keys,
    counts,
    pooled,
    pre_one,
    act_one,
    pre_two,
    back_two,
    back_one,
    row_sum,
    row_out,
    row_in,
    grad,
    part_out,
    part_in,
    part_all,
    weight_term,
    weight_sum,
    weight_out,
    weight_in,
    load_sem,
    gather_send,
    gather_recv,
    row_send,
    row_recv,
    part_send,
    part_recv,
    weight_send,
    weight_recv,
):
    looks = SLOTS * HOT
    batches, per_batch = label_ref.shape
    samples = batches * per_batch
    rows, width = table_ref.shape
    hidden = w_hid.shape[0]
    half = rows // HALVES
    me = {"shard": lax.axis_index("shard"), "grp": lax.axis_index("grp")}
    shard_bits = [("shard", b) for b in bits_of(n_shard)]
    grp_bits = [("grp", b) for b in bits_of(n_grp)]
    near, far = shard_bits[:1], shard_bits[1:]
    gather_order = [far[::-1] + near, far + near]
    row_order = near + far
    weight_order = near + far[::-1] + grp_bits

    def partner(step):
        axis, bit = step
        return {axis: flip(me[axis], bit)}

    load_in = pltpu.make_async_copy(w_in_hbm, w_in, load_sem.at[0])
    load_hid = pltpu.make_async_copy(w_hid_hbm, w_hid, load_sem.at[1])
    load_in.start()
    load_hid.start()

    barrier = pltpu.get_barrier_semaphore()
    peers = [("grp", relative) for relative in range(1, n_grp)]
    for step in shard_bits + peers:
        pl.semaphore_signal(barrier, inc=1, device_id=partner(step), device_id_type=MESH)
    for h in range(HALVES):
        gathered[h, 0] = table_ref[h * half : (h + 1) * half, :].astype(jnp.bfloat16)
    pl.semaphore_wait(barrier, len(shard_bits + peers))

    started = []

    def send(source, target, send_sem, recv_sem, step):
        copy = pltpu.make_async_remote_copy(
            src_ref=source,
            dst_ref=target,
            send_sem=send_sem,
            recv_sem=recv_sem,
            device_id=partner(step),
            device_id_type=MESH,
        )
        copy.start()
        started.append(copy)
        return copy

    def gather_step(i):
        return [
            send(
                gathered.at[h, pl.ds(0, 1 << i)],
                gathered.at[h, pl.ds(1 << i, 1 << i)],
                gather_send.at[h, i],
                gather_recv.at[h, i],
                gather_order[h][i],
            )
            for h in range(HALVES)
        ]

    in_flight = gather_step(0)

    ids = owner_ref[...] * rows + row_ref[...]
    for b in range(batches):
        turned_ids = jnp.transpose(ids[b * looks : (b + 1) * looks, :])
        for j in range(looks):
            keys[j, b * per_batch : (b + 1) * per_batch, :] = jnp.broadcast_to(
                turned_ids[:, j : j + 1], (per_batch, 128)
            ).astype(jnp.int16)

    lane = lax.broadcasted_iota(jnp.int32, (32, 128), 1)
    one = jnp.ones((32, 128), jnp.bfloat16)
    none = jnp.zeros((32, 128), jnp.bfloat16)

    def build(h, place):
        relative = low_first(gather_order[h], place)["shard"]
        first = flip(me["shard"], relative) * rows + h * half
        left = (h * n_shard + place) * half if keep else 0
        block = counts.at[:, left : left + half]
        lanes = [(lane + (first + c * 128)).astype(jnp.int16) for c in range(half // 128)]

        def tile(t, _):
            at = pl.ds(pl.multiple_of(t * 32, 32), 32)
            for s in range(SLOTS):
                into = pl.ds(pl.multiple_of(s * samples + t * 32, 32), 32)
                named = [keys[s * HOT + j, at, :] for j in range(HOT)]
                for c in range(half // 128):
                    hits = [jnp.where(k == lanes[c], one, none) for k in named]
                    total = (hits[0] + hits[1]) + (hits[2] + hits[3])
                    counts[into, left + c * 128 : left + (c + 1) * 128] = total
            return 0

        lax.fori_loop(0, samples // 32, tile, 0)
        return block

    places = [(h, p) for p in range(n_shard) for h in range(HALVES)]
    steps = len(shard_bits)
    if keep:
        share = len(places) // steps
        for i in range(steps):
            end = len(places) if i == steps - 1 else (i + 1) * share
            for h, p in places[i * share : end]:
                build(h, p)
            for copy in in_flight:
                copy.wait_recv()
            if i < steps - 1:
                in_flight = gather_step(i + 1)
        lookups = jnp.dot(
            counts[...],
            gathered[...].reshape(HALVES * n_shard * half, width),
            preferred_element_type=jnp.float32,
        )
    else:
        for i in range(steps):
            for copy in in_flight:
                copy.wait_recv()
            if i < steps - 1:
                in_flight = gather_step(i + 1)
        lookups = jnp.zeros((SLOTS * samples, width), jnp.float32)
        for h, p in places:
            lookups += jnp.dot(
                build(h, p)[...], gathered[h, p], preferred_element_type=jnp.float32
            )

    for s in range(SLOTS):
        pooled[:, s * width : (s + 1) * width] = lookups[
            s * samples : (s + 1) * samples
        ].astype(jnp.bfloat16)
    columns = [slice(c, c + TILE) for c in range(0, hidden, TILE)]
    load_in.wait()
    for c in columns:
        value = jnp.dot(pooled[...], w_in[:, c], preferred_element_type=jnp.float32)
        pre_one[:, c] = value
        act_one[:, c] = jnp.maximum(value, 0.0).astype(jnp.bfloat16)
    load_hid.wait()
    out_lines = w_out_ref[...].astype(jnp.float32)
    out_row = jnp.concatenate([out_lines[i : i + 1, :] for i in range(hidden // 128)], axis=1)
    terms = jnp.zeros((samples, TILE), jnp.float32)
    for c in columns:
        value = jnp.dot(act_one[...], w_hid[:, c], preferred_element_type=jnp.float32)
        pre_two[:, c] = value
        acted = jnp.maximum(value, 0.0).astype(jnp.bfloat16).astype(jnp.float32)
        terms = terms + acted * out_row[:, c]
    logits = jnp.broadcast_to(jnp.sum(terms, axis=1, keepdims=True), (samples, 128))
    label = label_ref[...].astype(jnp.float32)
    label_columns = []
    for b in range(batches):
        at = slice(b * per_batch, (b + 1) * per_batch)
        logit_ref[b : b + 1, :] = jnp.transpose(logits[at, :])[0:1, :]
        label_columns.append(
            jnp.transpose(jnp.broadcast_to(label[b : b + 1, :], (128, per_batch)))
        )
    slope = (jax.nn.sigmoid(logits) - jnp.concatenate(label_columns, axis=0))[:, 0:1]
    for c in columns:
        back_two[:, c] = jnp.where(pre_two[:, c] > 0, slope * out_row[:, c], 0.0).astype(
            jnp.bfloat16
        )
    across = (((1,), (1,)), ((), ()))
    for c in columns:
        value = lax.dot_general(
            back_two[...], w_hid[c, :], across, preferred_element_type=jnp.float32
        )
        back_one[:, c] = jnp.where(pre_one[:, c] > 0, value, 0.0).astype(jnp.bfloat16)

    turned = jnp.transpose(pooled[...].astype(jnp.float32)).astype(jnp.bfloat16)
    total_ref = weight_term if scatter else weight_ref
    for c in columns:
        total_ref[:, c] = jnp.dot(turned, back_one[:, c], preferred_element_type=jnp.float32)

    weight_steps = len(weight_order) if scatter else 0
    chunks = 1 << weight_steps

    def weight_step(i):
        count = chunks >> (i + 1)
        at = pl.ds(chunks - 2 * count, count)
        return send(
            weight_out.at[at],
            weight_in.at[at],
            weight_send.at[i],
            weight_recv.at[i],
            weight_order[i],
        )

    def weight_add(i, copy):
        copy.wait_recv()
        count = chunks >> (i + 1)
        base = chunks - 2 * count
        weight_sum[0:count] += weight_in[base : base + count].astype(jnp.float32)
        if i < weight_steps - 1:
            left = count // 2
            weight_out[chunks - count : chunks - left] = weight_sum[left:count].astype(
                jnp.bfloat16
            )
            return weight_step(i + 1)
        return None

    weight_copy = None
    if scatter:
        depth = weight_sum.shape[1]

        def chunk_of(place):
            relative = high_first(weight_order, place)
            index = flip(me["grp"], relative["grp"]) * n_shard + flip(
                me["shard"], relative["shard"]
            )
            return weight_term[pl.ds(pl.multiple_of(index * depth, depth), depth), :]

        kept = chunks // 2
        for p in range(kept):
            weight_out[p] = chunk_of(kept + p).astype(jnp.bfloat16)
        weight_copy = weight_step(0)
        for p in range(kept):
            weight_sum[p] = chunk_of(p)

    back_in = [
        lax.dot_general(
            back_one[...],
            w_in[s * width : (s + 1) * width, :],
            across,
            preferred_element_type=jnp.float32,
        )
        .astype(jnp.bfloat16)
        .astype(jnp.float32)
        for s in range(SLOTS)
    ]
    back_turned = jnp.transpose(jnp.concatenate(back_in, axis=0)).astype(jnp.bfloat16)

    where_in = [
        {low_first(gather_order[h], p)["shard"]: p for p in range(n_shard)}
        for h in range(HALVES)
    ]

    def row_term(place, h):
        p = where_in[h][high_first(row_order, place)["shard"]]
        left = (h * n_shard + p) * half
        block = counts.at[:, left : left + half] if keep else build(h, p)
        return jnp.dot(
            back_turned,
            block[...],
            preferred_element_type=jnp.float32,
        )

    def row_step(i):
        count = n_shard >> (i + 1)
        at = pl.ds(n_shard - 2 * count, count)
        return send(row_out.at[at], row_in.at[at], row_send.at[i], row_recv.at[i], row_order[i])

    def row_add(i, copy):
        copy.wait_recv()
        count = n_shard >> (i + 1)
        base = n_shard - 2 * count
        row_sum[0:count] += row_in[base : base + count].astype(jnp.float32)
        left = count // 2
        if i < len(row_order) - 1:
            row_out[n_shard - count : n_shard - left] = row_sum[left:count].astype(jnp.bfloat16)
            return row_step(i + 1)
        return group_send()

    part = rows // n_grp

    def rows_of(relative):
        at = flip(me["grp"], relative) * part
        return pl.ds(pl.multiple_of(at, part), part)

    def group_send():
        grad[...] = jnp.transpose(row_sum[0])
        copies = []
        for i, step in enumerate(peers):
            part_out[i] = grad[rows_of(step[1]), :].astype(jnp.bfloat16)
            copies.append(
                send(
                    part_out.at[i],
                    part_in.at[i],
                    part_send.at[0, i],
                    part_recv.at[0, i],
                    step,
                )
            )
        return copies

    def group_sum(copies):
        total = grad[rows_of(0), :]
        for i, copy in enumerate(copies):
            copy.wait_recv()
            total = total + part_in[i].astype(jnp.float32)
        part_all[0] = total.astype(jnp.bfloat16)
        return [
            send(
                part_all.at[0],
                part_all.at[step[1]],
                part_send.at[1, i],
                part_recv.at[1, i],
                step,
            )
            for i, step in enumerate(peers)
        ]

    kept = n_shard // 2
    for p in range(kept):
        for h in range(HALVES):
            row_out[p, :, h * half : (h + 1) * half] = row_term(kept + p, h).astype(jnp.bfloat16)
    row_copy = row_step(0)
    for p in range(kept):
        for h in range(HALVES):
            row_sum[p, :, h * half : (h + 1) * half] = row_term(p, h)

    for i in range(len(row_order)):
        if scatter:
            weight_copy = weight_add(i, weight_copy)
        row_copy = row_add(i, row_copy)
    weight_left = list(range(len(row_order), weight_steps))
    for i in weight_left[:1]:
        weight_copy = weight_add(i, weight_copy)
    row_copy = group_sum(row_copy)
    for i in weight_left[1:]:
        weight_copy = weight_add(i, weight_copy)

    if scatter:
        lines = hidden // 128
        for j in range(lines):
            weight_ref[pl.ds(j, depth, stride=lines), :] = weight_sum[
                0, :, j * 128 : (j + 1) * 128
            ]
    for i in range(n_grp):
        if i > 0:
            row_copy[i - 1].wait_recv()
        at = rows_of(i)
        term = part_all[i].astype(jnp.float32)
        new_sums = sums_ref[at, :] + term * term
        new_ref[at, :] = table_ref[at, :] - learn_rate * term / jnp.sqrt(new_sums)
    for copy in started:
        copy.wait_send()


def hand_over(*refs):
    sources, targets, sems = refs[:3], refs[3:6], refs[6]
    copies = [
        pltpu.make_async_copy(source, target, sems.at[i])
        for i, (source, target) in enumerate(zip(sources, targets))
    ]
    for copy in copies:
        copy.start()
    for copy in copies:
        copy.wait()


def local(
    n_shard,
    n_grp,
    owner_shard,
    local_row,
    click_label,
    row_table,
    squared_sums,
    w_input,
    w_hidden,
    w_output,
):
    rows, width = row_table.shape
    batches, per_batch, looks = local_row.shape
    samples = batches * per_batch
    wide, hidden = w_input.shape
    depth = wide // (n_shard * n_grp)
    scatter = depth > 0 and depth % 16 == 0
    keep = n_shard <= 8
    half = rows // HALVES
    chunks = n_shard * n_grp if scatter else 1
    depth = depth if scatter else 16
    shard_steps = n_shard.bit_length() - 1
    grp_steps = n_grp.bit_length() - 1
    part = rows // n_grp
    vmem = pl.BlockSpec(memory_space=pltpu.VMEM)
    hbm = pl.BlockSpec(memory_space=pl.ANY)
    low = jnp.bfloat16
    full = jnp.float32
    weight_shape = (depth * hidden // 128, 128) if scatter else (wide, hidden)
    new_table, logits, weight = pl.pallas_call(
        functools.partial(kernel, n_shard, n_grp, keep, scatter),
        out_shape=(
            jax.ShapeDtypeStruct((rows, width), full),
            jax.ShapeDtypeStruct((batches, per_batch), full),
            jax.ShapeDtypeStruct(weight_shape, full),
        ),
        in_specs=[vmem, vmem, vmem, vmem, vmem, hbm, hbm, vmem],
        out_specs=(vmem, vmem, vmem),
        scratch_shapes=[
            pltpu.VMEM((wide, hidden), low),
            pltpu.VMEM((hidden, hidden), low),
            pltpu.VMEM((HALVES, n_shard, half, width), low),
            pltpu.VMEM((looks, samples, 128), jnp.int16),
            pltpu.VMEM((SLOTS * samples, HALVES * n_shard * half if keep else half), low),
            pltpu.VMEM((samples, wide), low),
            pltpu.VMEM((samples, hidden), full),
            pltpu.VMEM((samples, hidden), low),
            pltpu.VMEM((samples, hidden), full),
            pltpu.VMEM((samples, hidden), low),
            pltpu.VMEM((samples, hidden), low),
            pltpu.VMEM((n_shard // 2, width, rows), full),
            pltpu.VMEM((n_shard - 1, width, rows), low),
            pltpu.VMEM((n_shard - 1, width, rows), low),
            pltpu.VMEM((rows, width), full),
            pltpu.VMEM((n_grp - 1, part, width), low),
            pltpu.VMEM((n_grp - 1, part, width), low),
            pltpu.VMEM((n_grp, part, width), low),
            pltpu.VMEM((wide, hidden) if scatter else (8, 128), full),
            pltpu.VMEM((max(1, chunks // 2), depth, hidden), full),
            pltpu.VMEM((max(1, chunks - 1), depth, hidden), low),
            pltpu.VMEM((max(1, chunks - 1), depth, hidden), low),
            pltpu.SemaphoreType.DMA((2,)),
            pltpu.SemaphoreType.DMA((HALVES, shard_steps)),
            pltpu.SemaphoreType.DMA((HALVES, shard_steps)),
            pltpu.SemaphoreType.DMA((shard_steps,)),
            pltpu.SemaphoreType.DMA((shard_steps,)),
            pltpu.SemaphoreType.DMA((2, n_grp - 1)),
            pltpu.SemaphoreType.DMA((2, n_grp - 1)),
            pltpu.SemaphoreType.DMA((shard_steps + grp_steps,)),
            pltpu.SemaphoreType.DMA((shard_steps + grp_steps,)),
        ],
        compiler_params=pltpu.CompilerParams(
            collective_id=0, has_side_effects=True, vmem_limit_bytes=56 * 1024 * 1024
        ),
    )(
        jnp.transpose(owner_shard, (0, 2, 3, 1)).reshape(batches * looks, per_batch),
        jnp.transpose(local_row, (0, 2, 1)).reshape(batches * looks, per_batch),
        click_label,
        row_table,
        squared_sums,
        w_input,
        w_hidden,
        w_output.reshape(hidden // 128, 128),
    )
    if scatter:
        new_table, logits, weight = pl.pallas_call(
            hand_over,
            out_shape=tuple(
                jax.ShapeDtypeStruct(a.shape, a.dtype) for a in (new_table, logits, weight)
            ),
            in_specs=[hbm, hbm, hbm],
            out_specs=(hbm, hbm, hbm),
            scratch_shapes=[pltpu.SemaphoreType.DMA((3,))],
            compiler_params=pltpu.CompilerParams(vmem_limit_bytes=60 * 1024 * 1024),
        )(new_table, logits, weight)
    weight = weight.reshape(-1)
    if not scatter:
        weight = lax.psum_scatter(weight, ("grp", "shard"), scatter_dimension=0, tiled=True)
    return (new_table, logits, weight)


def solution(mesh):
    in_specs = (
        P(None, ("grp", "shard"), None, None),
        P(None, ("grp", "shard"), None),
        P(None, ("grp", "shard")),
        P("shard", None),
        P("shard", None),
        P(),
        P(),
        P(),
    )
    out_specs = (P("shard", None), P(None, ("grp", "shard")), P(("grp", "shard")))
    part = functools.partial(local, mesh.shape["shard"], mesh.shape["grp"])
    return jax.shard_map(part, mesh=mesh, in_specs=in_specs, out_specs=out_specs, check_vma=False)
```
